768 devices in a mesh: blk: 48 (over y_hi, z), group: 16 (over y_lo, x, core).
Axes of the slice: x: 4, y: 8 (y_hi: 4, y_lo: 2; y = y_hi * 2 + y_lo), z: 12, core: 2. Of those that a mesh axis runs over, the one named last changes fastest.
Arguments:
- image_emb: bfloat16 [98304, 1152], P(('blk', 'group')), may hold values from -0.1875 to 0.1875
- text_feats: bfloat16 [98304, 1152], P(('blk', 'group')), may hold values from -0.75 to 0.75
- text_head: bfloat16 [1152, 1152], replicated, may hold values from -0.1875 to 0.1875
- scale_logarithm: float32 [1], replicated, may hold values from 1.6 to 2.6
- logit_bias: float32 [1], replicated, may hold values from -5 to -2
- pair_index: int32 [98304], P(('blk', 'group')), may hold values from 0 to 98303, as said below
Outputs:
- image_grad: float32 [98304, 1152], P(('blk', 'group'))
- text_grad: float32 [98304, 1152], P(('blk', 'group'))
- head_grad: float32 [1152, 1152], P('blk', 'group')
- row_loss: float32 [98304], P(('blk', 'group'))
The draws below stay inside these ranges and needn't reach their ends.
Inputs may be any that keep to these rules, and one draw needn't show every extreme that they name: `pair_index`: row r's pair id is r, or for some rows (r + 128), (r + 16 * 128) or (r + (16 + 1) * 128) modulo 98304.
All inputs are finite; a program needn't handle non-finite values.
Results may differ from the reference program's by a relative error of at most 0.022.
Values may be sent and summed in bfloat16 or wider, within the bound.
No kernel may reach another device: no remote copies, remote signals or barrier semaphores. Data moves between devices by JAX's collectives and lax.ppermute only.
A program may use at most 32 MiB of HBM per device.

```python
import jax
import jax.numpy as jnp
from jax import lax

D = 1152
B_DEV = 128
STEPS = 2
HOPS = 2
TOTAL = 98304
N_BLK = 48
N_GROUP = 16


def draw_pair_index(key, part):
    key = jax.random.fold_in(key, 7)
    first_key, second_key = jax.random.split(key)
    row_index = jnp.arange(TOTAL, dtype=jnp.int32)
    picked = jax.random.randint(first_key, (TOTAL,), 0, 4)
    which = jax.random.randint(second_key, (TOTAL,), 0, 3)
    offsets = jnp.where(which == 0, B_DEV, jnp.where(which == 1, N_GROUP * B_DEV, (N_GROUP + 1) * B_DEV)).astype(jnp.int32)
    shifted = (row_index + offsets) % TOTAL
    keeping = (picked != 0) | (row_index == 0) | (row_index == TOTAL - 1)
    return jnp.where(keeping, row_index, shifted).astype(jnp.int32)


def strengthened(drawn, own_key, source, target, parts, factor):
    owner, partner = [(jnp.arange(drawn.shape[axis_at]) // (drawn.shape[axis_at] // parts)).reshape([-1 if axis == axis_at else 1 for axis in range(drawn.ndim)]) for axis_at in (source, target)]
    chosen = jax.random.permutation(own_key, parts)[partner]
    strong = (owner == chosen) | (owner == (partner + parts // 2) % parts)
    return jnp.where(strong, factor * drawn, drawn)


def level_of(rng, shape, cuts, smallest, high):
    factor_of = 1.0
    for dim, shards_of in cuts:
        steps = jax.random.uniform(jax.random.fold_in(jax.random.fold_in(rng, 6), dim), (shards_of,), jnp.float32, smallest / len(cuts), high / len(cuts))
        factor_of = factor_of * jnp.repeat(jnp.exp(steps), shape[dim] // shards_of).reshape((-1,) + (1,) * (len(shape) - 1 - dim))
    return factor_of


def scatter_about(rng, shape, deviation, most, pieces=(), held_as=jnp.bfloat16):
    factor_of = level_of(rng, shape, pieces, -0.22, 0.18) if pieces else 1.0
    drawn = jax.random.normal(rng, shape, jnp.float32) * deviation * factor_of
    return jnp.minimum(jnp.maximum(drawn, -most), most).astype(held_as)


def heavy_noise(stream_key, shape, width, bound, pieces, heavy, kind=jnp.bfloat16):
    drawn = width * jax.random.normal(stream_key, shape, jnp.float32)
    if pieces:
        drawn = drawn * level_of(stream_key, shape, pieces, -0.22, 0.18)
    return jnp.clip(strengthened(drawn, jax.random.fold_in(stream_key, 3), *heavy), -bound, bound).astype(kind)


def setup_inputs(seed: int = 0) -> dict:
    keys = jax.random.split(jax.random.key(seed), 7)
    image_emb = scatter_about(keys[0], (TOTAL, D), D ** -0.5, 0.1875, ((0, 768),))
    text_feats = heavy_noise(keys[1], (TOTAL, D), D ** -0.5, 0.75, ((0, 768),), (0, 1, 384, 6.0))
    text_head = scatter_about(keys[2], (D, D), D ** -0.5, 0.1875)
    scale_logarithm = jnp.clip(jax.random.uniform(keys[3], (1,), jnp.float32, 1.6, 2.6), 1.6, 2.6)
    logit_bias = jnp.clip(jax.random.uniform(keys[4], (1,), jnp.float32, -5.0, -2.0), -5.0, -2.0)
    pair_index = draw_pair_index(jax.random.fold_in(keys[6], 71), 0)
    return {"image_emb": image_emb, "text_feats": text_feats, "text_head": text_head, "scale_logarithm": scale_logarithm, "logit_bias": logit_bias, "pair_index": pair_index}


EPS = 1e-06

def unit_rows(vectors):
    lengths = jnp.sqrt(lax.optimization_barrier(jnp.sum(vectors * vectors, axis=-1, keepdims=True)) + EPS)
    return (vectors / lengths, lengths)

def reference(image_emb, text_feats, text_head, scale_logarithm, logit_bias, pair_index):
    image_unit, image_len = unit_rows(image_emb.astype(jnp.float32))
    image_halfwide = image_unit.astype(jnp.bfloat16)
    text_pre = jnp.dot(text_feats, text_head, preferred_element_type=jnp.float32)
    text_unit, text_len = unit_rows(text_pre)
    text_bf = text_unit.astype(jnp.bfloat16)
    scale_factor = jnp.exp(scale_logarithm[0])
    logit_shift_bias = logit_bias[0]
    image_fullwide = image_halfwide.astype(jnp.float32).reshape(N_BLK, N_GROUP, B_DEV, D)
    text_four = text_bf.astype(jnp.float32).reshape(N_BLK, N_GROUP, B_DEV, D)
    row_ids = pair_index.reshape(N_BLK, N_GROUP, B_DEV)
    image_gradient = jnp.zeros((N_BLK, N_GROUP, B_DEV, D), jnp.float32)
    grad_text = jnp.zeros((N_BLK, N_GROUP, B_DEV, D), jnp.float32)
    loss_total = jnp.zeros((N_BLK, N_GROUP, B_DEV), jnp.float32)
    for hop_idx in range(HOPS):
        for step_idx in range(STEPS):
            visiting_text = jnp.roll(text_four, (step_idx, hop_idx), (0, 1))
            met_ids = jnp.roll(row_ids, (step_idx, hop_idx), (0, 1))
            unscaled_score = jnp.einsum('abid,abjd->abij', image_fullwide, visiting_text)
            logit_matrix = scale_factor * unscaled_score + logit_shift_bias
            target = jnp.where(row_ids[..., :, None] == met_ids[..., None, :], 1.0, -1.0).astype(jnp.float32)
            loss_total = loss_total + lax.optimization_barrier(jnp.sum(jax.nn.softplus(-target * logit_matrix), axis=-1))
            logit_gradient = (-target * jax.nn.sigmoid(-target * logit_matrix)).astype(jnp.bfloat16).astype(jnp.float32)
            image_gradient = image_gradient + scale_factor * jnp.einsum('kmcz,kmzu->kmcu', logit_gradient, visiting_text)
            partial_amount = scale_factor * jnp.einsum('txhw,txhp->txwp', logit_gradient, image_fullwide)
            grad_text = grad_text + jnp.roll(partial_amount, (-step_idx, -hop_idx), (0, 1))
    image_gradient = image_gradient.reshape(TOTAL, D)
    grad_text = grad_text.reshape(TOTAL, D)
    image_grad = (image_gradient - image_unit * lax.optimization_barrier(jnp.sum(image_unit * image_gradient, axis=-1, keepdims=True))) / image_len
    text_delta = ((grad_text - text_unit * lax.optimization_barrier(jnp.sum(text_unit * grad_text, axis=-1, keepdims=True))) / text_len).astype(jnp.bfloat16)
    text_grad = jnp.dot(text_delta, text_head.T, preferred_element_type=jnp.float32)
    head_grad = jnp.dot(text_feats.T, text_delta, preferred_element_type=jnp.float32)
    return (image_grad, text_grad, head_grad, loss_total.reshape(TOTAL))
```

```python
import jax
import jax.numpy as jnp
from jax import lax
from jax.experimental import pallas as pl
from jax.experimental.pallas import tpu as pltpu
from jax.sharding import Mesh
from jax.sharding import PartitionSpec as P

EPS = 1e-06
BF16 = jnp.bfloat16
F32 = jnp.float32
BLK = ("yh", "z")
GROUP = ("yl", "x", "core")
QUAD = ("yl", "core")
ALL = BLK + GROUP
N_YL, N_X, N_CORE = 2, 4, 2
TEXT_FLOPS = 12 * 10**9
VMEM_BYTES = 12 * 1024 * 1024


def shifted(value, axes, by):
    length = lax.axis_size(axes)
    return lax.ppermute(value, axes, [(i, (i + by) % length) for i in range(length)])


def kernel_call(kernel, out_shape, flops, scalars, arrays, scratch=()):
    moved = sum(v.size * v.dtype.itemsize for v in arrays)
    moved += sum(v.size * v.dtype.itemsize for v in jax.tree.leaves(out_shape))
    return pl.pallas_call(
        kernel,
        out_shape=out_shape,
        in_specs=[pl.BlockSpec(memory_space=pltpu.SMEM)] * len(scalars)
        + [pl.BlockSpec(memory_space=pltpu.VMEM)] * len(arrays),
        out_specs=jax.tree.map(lambda _: pl.BlockSpec(memory_space=pltpu.VMEM), out_shape),
        scratch_shapes=scratch,
        compiler_params=pltpu.CompilerParams(vmem_limit_bytes=VMEM_BYTES),
        cost_estimate=pl.CostEstimate(flops=flops, bytes_accessed=moved, transcendentals=0),
    )(*scalars, *arrays)


def dot_nt(left, right):
    return lax.dot_general(left, right, (((1,), (1,)), ((), ())), preferred_element_type=F32)


def lengths_of(vectors):
    return jnp.sqrt(jnp.sum(vectors * vectors, axis=-1, keepdims=True) + EPS)


def after(value, *earlier):
    return lax.optimization_barrier((value,) + earlier)[0]


def homes():
    n_group = N_YL * N_X * N_CORE
    n_blk = lax.axis_size("yh") * lax.axis_size("z")
    b = lax.axis_index("yh") * lax.axis_size("z") + lax.axis_index("z")
    g = (lax.axis_index("yl") * N_X + lax.axis_index("x")) * N_CORE + lax.axis_index("core")
    return b, g, n_blk, n_group


def offsets_of(ids):
    b, g, n_blk, n_group = homes()
    rows = ids.shape[1]
    total = n_blk * n_group * rows
    own = (b * n_group + g) * rows + lax.broadcasted_iota(jnp.int32, ids.shape, 1)
    step = ids - own
    step = jnp.where(step < 0, step + total, step)
    code = jnp.where(step == 0, 0.0, float(n_group + 1))
    code = jnp.where(step == rows, 1.0, code)
    return jnp.where(step == n_group * rows, float(n_group), code)


def with_offsets(units, ids):
    code = jnp.broadcast_to(offsets_of(ids), (8, ids.shape[1]))
    rest = jnp.zeros((8, units.shape[1] - ids.shape[1]), F32)
    return jnp.concatenate([units, jnp.concatenate([code, rest], axis=1)], axis=0).astype(BF16)


def split_block(block):
    rows = block.shape[0] - 8
    code = block[...].astype(F32)[rows : rows + 1, 0:rows]
    return block[0:rows, :], code


def met_pairs(image_code, text_code, apart, total):
    rows = image_code.shape[1]
    row = lax.broadcasted_iota(jnp.int32, (rows, rows), 0)
    column = lax.broadcasted_iota(jnp.int32, (rows, rows), 1)
    step = image_code - text_code + apart.astype(F32)
    same = (step == 0.0) | (step == float(total)) | (step == -float(total))
    return (row == column) & same


def signed_logit(score, match, scale, bias):
    logit = scale * score + bias
    return jnp.where(match, -logit, logit)


def slope_of(value, match):
    slope = 1.0 / (1.0 + jnp.exp(-value))
    return jnp.where(match, -slope, slope).astype(BF16)


def softplus(value):
    return jnp.maximum(value, 0.0) + jnp.log1p(jnp.exp(-jnp.abs(value)))


def block_kernel(img, feats, ids, img_block, txt_block):
    wide = img[...].astype(F32)
    img_block[...] = with_offsets(wide / lengths_of(wide), ids[...])
    txt_block[...] = with_offsets(feats[...].astype(F32), ids[...])


def text_kernel(feats, head, unit, length):
    pre = jnp.dot(feats[...], head[...], preferred_element_type=F32)
    size = lengths_of(pre)
    unit[...] = pre / size
    length[...] = size


def text_side_kernel(scale_log, logit_bias, unit, length, img, img_g, img_b, img_bg, turned):
    scale = jnp.exp(jnp.full((1, 1), scale_log[0], F32))
    bias = logit_bias[0]
    b, g, n_blk, n_group = homes()
    next_b = lax.rem(b + 1, n_blk) - b
    next_g = lax.rem(g + 1, n_group) - g
    aparts = (0 * b, next_g, next_b * n_group, next_b * n_group + next_g)
    own = unit[...]
    text = own.astype(BF16)
    total = jnp.zeros(own.shape, F32)
    own_code = split_block(img)[1]
    for block, apart in zip((img, img_g, img_b, img_bg), aparts):
        images, code = split_block(block)
        match = met_pairs(code, own_code, apart, n_blk * n_group)
        value = signed_logit(dot_nt(text, images), match, scale, bias)
        total += jnp.dot(slope_of(value, match), images, preferred_element_type=F32)
    grad = scale * total
    result = (grad - own * jnp.sum(own * grad, axis=-1, keepdims=True)) / length[...]
    columns = result.T
    part = columns.shape[0] // (N_YL * N_X * N_CORE)
    for yl in range(N_YL):
        for x in range(N_X):
            for core in range(N_CORE):
                at = ((yl * N_X + x) * N_CORE + core) * part
                turned[(yl * N_CORE + core) * N_X + x] = columns[at : at + part].astype(BF16)


def image_side_kernel(
    scale_log,
    logit_bias,
    img,
    unit,
    txt,
    txt_g,
    txt_b,
    txt_bg,
    turned,
    head,
    grad_out,
    loss_out,
    text_out,
):
    scale = jnp.exp(jnp.full((1, 1), scale_log[0], F32))
    bias = logit_bias[0]
    b, g, n_blk, n_group = homes()
    last_b = b - lax.rem(b + n_blk - 1, n_blk)
    last_g = g - lax.rem(g + n_group - 1, n_group)
    aparts = (0 * b, last_g, last_b * n_group, last_b * n_group + last_g)
    wide = img[...].astype(F32)
    size = lengths_of(wide)
    own = wide / size
    image = own.astype(BF16)
    total = jnp.zeros(wide.shape, F32)
    loss = jnp.zeros((wide.shape[0], 1), F32)
    own_code = split_block(txt)[1]
    for block, apart in zip((txt, txt_g, txt_b, txt_bg), aparts):
        feats, code = split_block(block)
        if block is txt:
            texts = unit[...].astype(BF16)
        else:
            pre = jnp.dot(feats, head[...], preferred_element_type=F32)
            texts = (pre / lengths_of(pre)).astype(BF16)
        match = met_pairs(own_code, code, apart, n_blk * n_group)
        value = signed_logit(dot_nt(image, texts), match, scale, bias)
        loss += jnp.sum(softplus(value), axis=-1, keepdims=True)
        total += jnp.dot(slope_of(value, match), texts, preferred_element_type=F32)
    grad = scale * total
    grad_out[...] = (grad - own * jnp.sum(own * grad, axis=-1, keepdims=True)) / size
    loss_out[...] = jnp.broadcast_to(loss, (loss.shape[0], loss.shape[0])).T[0:1]
    blocks = [
        turned[(yl * N_CORE + core) * N_X + x].astype(F32)
        for yl in range(N_YL)
        for x in range(N_X)
        for core in range(N_CORE)
    ]
    delta = jnp.concatenate(blocks, axis=0).T.astype(BF16)
    text_out[...] = dot_nt(delta, head[...])


def head_kernel(place, met, feats, feats_c, feats_y, feats_cy, out):
    m = place[0]
    across = m + 1 - 2 * lax.rem(m, 2)
    total = jnp.zeros((met.shape[1] * met.shape[2], feats.shape[1]), F32)
    for at, block in (
        (m, feats),
        (across, feats_c),
        (lax.rem(m + 2, 4), feats_y),
        (lax.rem(across + 2, 4), feats_cy),
    ):
        columns = met[at].astype(F32).reshape(total.shape[0], met.shape[3]).astype(BF16)
        total += jnp.dot(columns, block[...], preferred_element_type=F32)
    out[...] = total.reshape(out.shape).astype(BF16)


def pack_kernel(parts, out, wide, tail, packed):
    columns = jnp.sum(parts[...].astype(F32), axis=0)
    n, depth, lanes = wide.shape
    width = columns.shape[0]
    over = lanes - width
    left = width - over
    half = depth // 2
    wide[...] = jnp.concatenate([columns, columns[:over]], axis=0).T.reshape(wide.shape)
    copies = [columns[over:]] * (lanes // left)
    tail[...] = jnp.concatenate(copies, axis=0).T.reshape(tail.shape)
    lane = lax.broadcasted_iota(jnp.int32, (n, half, lanes), 2)
    packed[:, 0:half, :] = jnp.where(lane < width, wide[:, 0:half, :], wide[:, half:depth, :])
    short = half // 3
    lane = lax.broadcasted_iota(jnp.int32, (n, short, lanes), 2)
    rest = tail[:, half : half + short, :]
    for k in (1, 2):
        piece = tail[:, half + k * short : half + (k + 1) * short, :]
        rest = jnp.where(lane >= k * left, piece, rest)
    packed[:, half : half + short, :] = rest
    out[...] = packed[...].astype(BF16)


def unpack_kernel(parts, out):
    total = jnp.sum(parts[...].astype(F32), axis=0)
    depth, width = out.shape
    lanes = total.shape[1]
    over = lanes - width
    left = width - over
    half = depth // 2
    short = half // 3
    out[0:half, :] = total[0:half, 0:width]
    out[half:depth, 0:over] = total[0:half, width:lanes]
    for k in range(3):
        at = half + k * short
        out[at : at + short, over:width] = total[half : half + short, k * left : (k + 1) * left]


def body(image_emb, text_feats, text_head, scale_log, logit_bias, pair_index):
    rows, width = image_emb.shape
    n_blk = lax.axis_size(BLK)
    ids = pair_index.reshape(1, rows)
    like = jax.ShapeDtypeStruct
    score = 2 * rows * rows * width

    block = like((rows + 8, width), BF16)
    img, txt = kernel_call(block_kernel, (block, block), 0, (), (image_emb, text_feats, ids))
    img_b = shifted(img, BLK, -1)
    txt_b = shifted(txt, BLK, 1)
    img_g = shifted(img, GROUP, -1)
    txt_g = shifted(after(txt, img_g), GROUP, 1)
    unit, length = kernel_call(
        text_kernel,
        (like((rows, width), F32), like((rows, 1), F32)),
        TEXT_FLOPS,
        (),
        (after(text_feats, img_g), text_head),
    )
    img_b, txt_b = lax.optimization_barrier((img_b, txt_b, unit, txt_g))[:2]
    img_bg = shifted(img_b, GROUP, -1)
    swap = [(0, 1), (1, 0)]
    feats_y = lax.ppermute(after(text_feats, img_b), "yl", swap)

    part = width // (N_YL * N_X * N_CORE)
    turned = kernel_call(
        text_side_kernel,
        like((N_YL * N_CORE * N_X, part, rows), BF16),
        8 * score,
        (scale_log, logit_bias),
        (unit, length, img, img_g, img_b, img_bg),
    )

    late_txt, late_b = lax.optimization_barrier((text_feats, txt_b, turned))[:2]
    feats_c = lax.ppermute(late_txt, "core", swap)
    feats_cy = lax.ppermute(feats_y, "core", swap)
    txt_bg = shifted(late_b, GROUP, 1)
    place = lax.axis_index(QUAD).reshape(1)
    quads = turned.reshape(N_YL * N_CORE, N_X, part, rows)
    met = lax.all_to_all(quads, QUAD, 0, 0)
    partial = kernel_call(
        head_kernel,
        like((N_X, part, width), BF16),
        2 * 4 * rows * width * N_X * part,
        (place,),
        (met, text_feats, feats_c, feats_y, feats_cy),
    )
    partial = lax.all_to_all(after(partial, txt_bg), "x", 0, 0)
    depth = width // n_blk
    packed = kernel_call(
        pack_kernel,
        like((n_blk, 16, 128), BF16),
        0,
        (),
        (partial,),
        (
            pltpu.VMEM((n_blk, depth, 128), F32),
            pltpu.VMEM((n_blk, depth, 128), F32),
            pltpu.VMEM((n_blk, 16, 128), F32),
        ),
    )
    summed = lax.all_to_all(packed, BLK, 0, 0)
    head_grad = kernel_call(unpack_kernel, like((depth, part), F32), 0, (), (summed,))

    image_grad, row_loss, text_grad = kernel_call(
        image_side_kernel,
        (like((rows, width), F32), like((1, rows), F32), like((rows, width), F32)),
        8 * score + 8 * rows * width * width,
        (scale_log, logit_bias),
        (
            after(image_emb, packed),
            unit,
            txt,
            txt_g,
            txt_b,
            txt_bg,
            turned,
            text_head,
        ),
    )
    return (image_grad, text_grad, head_grad, row_loss.reshape(rows))


def solution(mesh):
    fine = Mesh(mesh.devices.reshape(4, 12, N_YL, N_X, N_CORE), ALL)
    rows = P(ALL, None)
    return jax.shard_map(
        body,
        mesh=fine,
        in_specs=(rows, rows, P(), P(), P(), P(ALL)),
        out_specs=(rows, rows, P(BLK, GROUP), P(ALL)),
        check_vma=False,
    )
```

```python
import jax
import jax.numpy as jnp
from jax import lax
from jax.experimental import pallas as pl
from jax.experimental.pallas import tpu as pltpu
from jax.sharding import Mesh
from jax.sharding import PartitionSpec as P

EPS = 1e-06
BF16 = jnp.bfloat16
F32 = jnp.float32
BLK = ("yh", "z")
GROUP = ("yl", "x", "core")
QUAD = ("yl", "core")
ALL = BLK + GROUP
N_YL, N_X, N_CORE = 2, 4, 2
TEXT_FLOPS = 12 * 10**9
VMEM_BYTES = 12 * 1024 * 1024


def shifted(value, axes, by):
    length = lax.axis_size(axes)
    return lax.ppermute(value, axes, [(i, (i + by) % length) for i in range(length)])


def kernel_call(kernel, out_shape, flops, scalars, arrays, scratch=(), vmem=VMEM_BYTES):
    moved = sum(v.size * v.dtype.itemsize for v in arrays)
    moved += sum(v.size * v.dtype.itemsize for v in jax.tree.leaves(out_shape))
    return pl.pallas_call(
        kernel,
        out_shape=out_shape,
        in_specs=[pl.BlockSpec(memory_space=pltpu.SMEM)] * len(scalars)
        + [pl.BlockSpec(memory_space=pltpu.VMEM)] * len(arrays),
        out_specs=jax.tree.map(lambda _: pl.BlockSpec(memory_space=pltpu.VMEM), out_shape),
        scratch_shapes=scratch,
        compiler_params=pltpu.CompilerParams(vmem_limit_bytes=vmem),
        cost_estimate=pl.CostEstimate(flops=flops, bytes_accessed=moved, transcendentals=0),
    )(*scalars, *arrays)


def dot_nt(left, right):
    return lax.dot_general(left, right, (((1,), (1,)), ((), ())), preferred_element_type=F32)


def lengths_of(vectors):
    return jnp.sqrt(jnp.sum(vectors * vectors, axis=-1, keepdims=True) + EPS)


def after(value, *earlier):
    return lax.optimization_barrier((value,) + earlier)[0]


def homes():
    n_group = N_YL * N_X * N_CORE
    n_blk = lax.axis_size("yh") * lax.axis_size("z")
    b = lax.axis_index("yh") * lax.axis_size("z") + lax.axis_index("z")
    g = (lax.axis_index("yl") * N_X + lax.axis_index("x")) * N_CORE + lax.axis_index("core")
    return b, g, n_blk, n_group


def offsets_of(ids):
    b, g, n_blk, n_group = homes()
    rows = ids.shape[1]
    total = n_blk * n_group * rows
    own = (b * n_group + g) * rows + lax.broadcasted_iota(jnp.int32, ids.shape, 1)
    step = ids - own
    step = jnp.where(step < 0, step + total, step)
    code = jnp.where(step == 0, 0.0, float(n_group + 1))
    code = jnp.where(step == rows, 1.0, code)
    return jnp.where(step == n_group * rows, float(n_group), code)


def with_offsets(units, ids):
    code = jnp.broadcast_to(offsets_of(ids), (8, ids.shape[1]))
    rest = jnp.zeros((8, units.shape[1] - ids.shape[1]), F32)
    return jnp.concatenate([units, jnp.concatenate([code, rest], axis=1)], axis=0).astype(BF16)


def split_block(block):
    rows = block.shape[0] - 8
    code = block[...].astype(F32)[rows : rows + 1, 0:rows]
    return block[0:rows, :], code


def met_pairs(image_code, text_code, apart, total):
    rows = image_code.shape[1]
    row = lax.broadcasted_iota(jnp.int32, (rows, rows), 0)
    column = lax.broadcasted_iota(jnp.int32, (rows, rows), 1)
    step = image_code - text_code + apart.astype(F32)
    same = (step == 0.0) | (step == float(total)) | (step == -float(total))
    return (row == column) & same


def signed_logit(score, match, scale, bias):
    logit = scale * score + bias
    return jnp.where(match, -logit, logit)


def slope_of(value, match):
    slope = 1.0 / (1.0 + jnp.exp(-value))
    return jnp.where(match, -slope, slope).astype(BF16)


def softplus(value):
    return jnp.maximum(value, 0.0) + jnp.log1p(jnp.exp(-jnp.abs(value)))


def block_kernel(img, feats, ids, img_block, txt_block):
    wide = img[...].astype(F32)
    img_block[...] = with_offsets(wide / lengths_of(wide), ids[...])
    txt_block[...] = with_offsets(feats[...].astype(F32), ids[...])


def text_kernel(feats, head, unit, length):
    pre = jnp.dot(feats[...], head[...], preferred_element_type=F32)
    size = lengths_of(pre)
    unit[...] = pre / size
    length[...] = size


def text_side_kernel(scale_log, logit_bias, unit, length, img, img_g, img_b, img_bg, turned):
    scale = jnp.exp(jnp.full((1, 1), scale_log[0], F32))
    bias = logit_bias[0]
    b, g, n_blk, n_group = homes()
    next_b = lax.rem(b + 1, n_blk) - b
    next_g = lax.rem(g + 1, n_group) - g
    aparts = (0 * b, next_g, next_b * n_group, next_b * n_group + next_g)
    own = unit[...]
    text = own.astype(BF16)
    total = jnp.zeros(own.shape, F32)
    own_code = split_block(img)[1]
    for block, apart in zip((img, img_g, img_b, img_bg), aparts):
        images, code = split_block(block)
        match = met_pairs(code, own_code, apart, n_blk * n_group)
        value = signed_logit(dot_nt(text, images), match, scale, bias)
        total += jnp.dot(slope_of(value, match), images, preferred_element_type=F32)
    grad = scale * total
    result = (grad - own * jnp.sum(own * grad, axis=-1, keepdims=True)) / length[...]
    columns = result.T
    part = columns.shape[0] // (N_YL * N_X * N_CORE)
    for yl in range(N_YL):
        for x in range(N_X):
            for core in range(N_CORE):
                at = ((yl * N_X + x) * N_CORE + core) * part
                turned[(yl * N_CORE + core) * N_X + x] = columns[at : at + part].astype(BF16)


def image_pairs(scale, bias, image, own_code, texts, code, apart, total):
    match = met_pairs(own_code, code, apart, total)
    value = signed_logit(dot_nt(image, texts), match, scale, bias)
    loss = jnp.sum(softplus(value), axis=-1, keepdims=True)
    return jnp.dot(slope_of(value, match), texts, preferred_element_type=F32), loss


def text_rows(feats, head):
    pre = jnp.dot(feats, head[...], preferred_element_type=F32)
    return (pre / lengths_of(pre)).astype(BF16)


def image_side_kernel(
    scale_log, logit_bias, img, unit, txt, txt_g, txt_b, turned, head, grad_out, loss_out, text_out
):
    scale = jnp.exp(jnp.full((1, 1), scale_log[0], F32))
    bias = logit_bias[0]
    b, g, n_blk, n_group = homes()
    last_b = b - lax.rem(b + n_blk - 1, n_blk)
    last_g = g - lax.rem(g + n_group - 1, n_group)
    image, _ = split_block(img)
    _, own_code = split_block(txt)
    grad, loss = image_pairs(
        scale, bias, image, own_code, unit[...].astype(BF16), own_code, 0 * b, n_blk * n_group
    )
    for block, apart in ((txt_g, last_g), (txt_b, last_b * n_group)):
        feats, code = split_block(block)
        more, lost = image_pairs(
            scale, bias, image, own_code, text_rows(feats, head), code, apart, n_blk * n_group
        )
        grad += more
        loss += lost
    grad_out[...] = grad
    loss_out[...] = loss
    blocks = [
        turned[(yl * N_CORE + core) * N_X + x].astype(F32)
        for yl in range(N_YL)
        for x in range(N_X)
        for core in range(N_CORE)
    ]
    delta = jnp.concatenate(blocks, axis=0).T.astype(BF16)
    text_out[...] = dot_nt(delta, head[...])


def diagonal_kernel(
    scale_log, logit_bias, raw, img, txt, txt_bg, head, grad_in, loss_in, grad_out, loss_out
):
    scale = jnp.exp(jnp.full((1, 1), scale_log[0], F32))
    bias = logit_bias[0]
    b, g, n_blk, n_group = homes()
    last_b = b - lax.rem(b + n_blk - 1, n_blk)
    last_g = g - lax.rem(g + n_group - 1, n_group)
    image, _ = split_block(img)
    _, own_code = split_block(txt)
    feats, code = split_block(txt_bg)
    apart = last_b * n_group + last_g
    more, lost = image_pairs(
        scale, bias, image, own_code, text_rows(feats, head), code, apart, n_blk * n_group
    )
    grad = scale * (grad_in[...] + more)
    wide = raw[...].astype(F32)
    size = lengths_of(wide)
    own = wide / size
    grad_out[...] = (grad - own * jnp.sum(own * grad, axis=-1, keepdims=True)) / size
    loss = loss_in[...] + lost
    loss_out[...] = jnp.broadcast_to(loss, (loss.shape[0], loss.shape[0])).T[0:1]


def head_kernel(place, met, feats, feats_c, feats_y, feats_cy, out):
    m = place[0]
    across = m + 1 - 2 * lax.rem(m, 2)
    total = jnp.zeros((met.shape[1] * met.shape[2], feats.shape[1]), F32)
    for at, block in (
        (m, feats),
        (across, feats_c),
        (lax.rem(m + 2, 4), feats_y),
        (lax.rem(across + 2, 4), feats_cy),
    ):
        columns = met[at].astype(F32).reshape(total.shape[0], met.shape[3]).astype(BF16)
        total += jnp.dot(columns, block[...], preferred_element_type=F32)
    out[...] = total.reshape(out.shape).astype(BF16)


def pack_kernel(parts, out, wide, tail, packed):
    columns = jnp.sum(parts[...].astype(F32), axis=0)
    n, depth, lanes = wide.shape
    width = columns.shape[0]
    over = lanes - width
    left = width - over
    half = depth // 2
    wide[...] = jnp.concatenate([columns, columns[:over]], axis=0).T.reshape(wide.shape)
    copies = [columns[over:]] * (lanes // left)
    tail[...] = jnp.concatenate(copies, axis=0).T.reshape(tail.shape)
    lane = lax.broadcasted_iota(jnp.int32, (n, half, lanes), 2)
    packed[:, 0:half, :] = jnp.where(lane < width, wide[:, 0:half, :], wide[:, half:depth, :])
    short = half // 3
    lane = lax.broadcasted_iota(jnp.int32, (n, short, lanes), 2)
    rest = tail[:, half : half + short, :]
    for k in (1, 2):
        piece = tail[:, half + k * short : half + (k + 1) * short, :]
        rest = jnp.where(lane >= k * left, piece, rest)
    packed[:, half : half + short, :] = rest
    out[...] = packed[...].astype(BF16)


def unpack_kernel(parts, out):
    total = jnp.sum(parts[...].astype(F32), axis=0)
    depth, width = out.shape
    lanes = total.shape[1]
    over = lanes - width
    left = width - over
    half = depth // 2
    short = half // 3
    out[0:half, :] = total[0:half, 0:width]
    out[half:depth, 0:over] = total[0:half, width:lanes]
    for k in range(3):
        at = half + k * short
        out[at : at + short, over:width] = total[half : half + short, k * left : (k + 1) * left]


def body(image_emb, text_feats, text_head, scale_log, logit_bias, pair_index):
    rows, width = image_emb.shape
    n_blk = lax.axis_size(BLK)
    ids = pair_index.reshape(1, rows)
    like = jax.ShapeDtypeStruct
    score = 2 * rows * rows * width

    block = like((rows + 8, width), BF16)
    img, txt = kernel_call(
        block_kernel, (block, block), 0, (), (image_emb, text_feats, ids), vmem=60 * 1024 * 1024
    )
    img_b = shifted(img, BLK, -1)
    txt_b = shifted(txt, BLK, 1)
    swap = [(0, 1), (1, 0)]
    unit, length = kernel_call(
        text_kernel,
        (like((rows, width), F32), like((rows, 1), F32)),
        TEXT_FLOPS,
        (),
        (after(text_feats, img), text_head),
    )
    late_img, late_txt, late_feats = lax.optimization_barrier((img, txt, text_feats, unit))[:3]
    img_g = shifted(late_img, GROUP, -1)
    txt_g = shifted(late_txt, GROUP, 1)
    feats_c = lax.ppermute(late_feats, "core", swap)
    img_b, txt_b = lax.optimization_barrier((img_b, txt_b, unit, feats_c))[:2]
    img_bg = shifted(img_b, GROUP, -1)
    feats_y = lax.ppermute(after(text_feats, img_b), "yl", swap)

    part = width // (N_YL * N_X * N_CORE)
    turned = kernel_call(
        text_side_kernel,
        like((N_YL * N_CORE * N_X, part, rows), BF16),
        8 * score,
        (scale_log, logit_bias),
        (after(unit, txt_g), length, img, img_g, img_b, img_bg),
    )

    feats_cy = lax.ppermute(feats_y, "core", swap)
    place = lax.axis_index(QUAD).reshape(1)
    quads = turned.reshape(N_YL * N_CORE, N_X, part, rows)
    met = lax.all_to_all(quads, QUAD, 0, 0)
    products = kernel_call(
        head_kernel,
        like((N_X, part, width), BF16),
        2 * 4 * rows * width * N_X * part,
        (place,),
        (met, text_feats, feats_c, feats_y, feats_cy),
    )
    partial = lax.all_to_all(products, "x", 0, 0)
    part_grad, part_loss, text_grad = kernel_call(
        image_side_kernel,
        (like((rows, width), F32), like((rows, 1), F32), like((rows, width), F32)),
        24 * score + 24 * rows * width * width,
        (scale_log, logit_bias),
        (after(img, products), unit, txt, txt_g, txt_b, turned, text_head),
    )
    depth = width // n_blk
    packed = kernel_call(
        pack_kernel,
        like((n_blk, 16, 128), BF16),
        0,
        (),
        (partial,),
        (
            pltpu.VMEM((n_blk, depth, 128), F32),
            pltpu.VMEM((n_blk, depth, 128), F32),
            pltpu.VMEM((n_blk, 16, 128), F32),
        ),
    )
    packed = after(packed, part_loss)
    summed = lax.all_to_all(packed, BLK, 0, 0)
    txt_bg = shifted(after(txt_b, packed), GROUP, 1)
    head_grad = kernel_call(unpack_kernel, like((depth, part), F32), 0, (), (summed,))

    image_grad, row_loss = kernel_call(
        diagonal_kernel,
        (like((rows, width), F32), like((1, rows), F32)),
        12 * score + 12 * rows * width * width,
        (scale_log, logit_bias),
        (image_emb, img, txt, txt_bg, text_head, part_grad, part_loss),
    )
    return (image_grad, text_grad, head_grad, row_loss.reshape(rows))


def solution(mesh):
    fine = Mesh(mesh.devices.reshape(4, 12, N_YL, N_X, N_CORE), ALL)
    rows = P(ALL, None)
    return jax.shard_map(
        body,
        mesh=fine,
        in_specs=(rows, rows, P(), P(), P(), P(ALL)),
        out_specs=(rows, rows, P(BLK, GROUP), P(ALL)),
        check_vma=False,
    )
```

```python
import jax
import jax.numpy as jnp
from jax import lax
from jax.experimental import pallas as pl
from jax.experimental.pallas import tpu as pltpu
from jax.sharding import Mesh
from jax.sharding import PartitionSpec as P

EPS = 1e-06
BF16 = jnp.bfloat16
F32 = jnp.float32
BLK = ("yh", "z")
GROUP = ("yl", "x", "core")
QUAD = ("yl", "core")
ALL = BLK + GROUP
N_YL, N_X, N_CORE = 2, 4, 2
TEXT_FLOPS = 12 * 10**9
VMEM_BYTES = 12 * 1024 * 1024


def shifted(value, axes, by):
    length = lax.axis_size(axes)
    return lax.ppermute(value, axes, [(i, (i + by) % length) for i in range(length)])


def kernel_call(kernel, out_shape, flops, scalars, arrays, scratch=(), vmem=VMEM_BYTES):
    moved = sum(v.size * v.dtype.itemsize for v in arrays)
    moved += sum(v.size * v.dtype.itemsize for v in jax.tree.leaves(out_shape))
    return pl.pallas_call(
        kernel,
        out_shape=out_shape,
        in_specs=[pl.BlockSpec(memory_space=pltpu.SMEM)] * len(scalars)
        + [pl.BlockSpec(memory_space=pltpu.VMEM)] * len(arrays),
        out_specs=jax.tree.map(lambda _: pl.BlockSpec(memory_space=pltpu.VMEM), out_shape),
        scratch_shapes=scratch,
        compiler_params=pltpu.CompilerParams(vmem_limit_bytes=vmem),
        cost_estimate=pl.CostEstimate(flops=flops, bytes_accessed=moved, transcendentals=0),
    )(*scalars, *arrays)


def dot_nt(left, right):
    return lax.dot_general(left, right, (((1,), (1,)), ((), ())), preferred_element_type=F32)


def lengths_of(vectors):
    return jnp.sqrt(jnp.sum(vectors * vectors, axis=-1, keepdims=True) + EPS)


def after(value, *earlier):
    return lax.optimization_barrier((value,) + earlier)[0]


def homes():
    n_group = N_YL * N_X * N_CORE
    n_blk = lax.axis_size("yh") * lax.axis_size("z")
    b = lax.axis_index("yh") * lax.axis_size("z") + lax.axis_index("z")
    g = (lax.axis_index("yl") * N_X + lax.axis_index("x")) * N_CORE + lax.axis_index("core")
    return b, g, n_blk, n_group


def offsets_of(ids):
    b, g, n_blk, n_group = homes()
    rows = ids.shape[1]
    total = n_blk * n_group * rows
    own = (b * n_group + g) * rows + lax.broadcasted_iota(jnp.int32, ids.shape, 1)
    step = ids - own
    step = jnp.where(step < 0, step + total, step)
    code = jnp.where(step == 0, 0.0, float(n_group + 1))
    code = jnp.where(step == rows, 1.0, code)
    return jnp.where(step == n_group * rows, float(n_group), code)


def with_offsets(units, ids):
    code = jnp.broadcast_to(offsets_of(ids), (8, ids.shape[1]))
    rest = jnp.zeros((8, units.shape[1] - ids.shape[1]), F32)
    return jnp.concatenate([units, jnp.concatenate([code, rest], axis=1)], axis=0).astype(BF16)


def split_block(block):
    rows = block.shape[0] - 8
    code = block[...].astype(F32)[rows : rows + 1, 0:rows]
    return block[0:rows, :], code


def met_pairs(image_code, text_code, apart, total):
    rows = image_code.shape[1]
    row = lax.broadcasted_iota(jnp.int32, (rows, rows), 0)
    column = lax.broadcasted_iota(jnp.int32, (rows, rows), 1)
    step = image_code - text_code + apart.astype(F32)
    same = (step == 0.0) | (step == float(total)) | (step == -float(total))
    return (row == column) & same


def signed_logit(score, match, scale, bias):
    logit = scale * score + bias
    return jnp.where(match, -logit, logit)


def slope_of(value, match):
    slope = 1.0 / (1.0 + jnp.exp(-value))
    return jnp.where(match, -slope, slope).astype(BF16)


def softplus(value):
    return jnp.maximum(value, 0.0) + jnp.log1p(jnp.exp(-jnp.abs(value)))


def block_kernel(img, feats, ids, img_block, txt_block):
    wide = img[...].astype(F32)
    img_block[...] = with_offsets(wide / lengths_of(wide), ids[...])
    txt_block[...] = with_offsets(feats[...].astype(F32), ids[...])


def text_kernel(feats, head, unit, length):
    pre = jnp.dot(feats[...], head[...], preferred_element_type=F32)
    size = lengths_of(pre)
    unit[...] = pre / size
    length[...] = size


def text_side_kernel(scale_log, logit_bias, unit, length, img, img_g, img_b, img_bg, turned):
    scale = jnp.exp(jnp.full((1, 1), scale_log[0], F32))
    bias = logit_bias[0]
    b, g, n_blk, n_group = homes()
    next_b = lax.rem(b + 1, n_blk) - b
    next_g = lax.rem(g + 1, n_group) - g
    aparts = (0 * b, next_g, next_b * n_group, next_b * n_group + next_g)
    own = unit[...]
    text = own.astype(BF16)
    total = jnp.zeros(own.shape, F32)
    own_code = split_block(img)[1]
    for block, apart in zip((img, img_g, img_b, img_bg), aparts):
        images, code = split_block(block)
        match = met_pairs(code, own_code, apart, n_blk * n_group)
        value = signed_logit(dot_nt(text, images), match, scale, bias)
        total += jnp.dot(slope_of(value, match), images, preferred_element_type=F32)
    grad = scale * total
    result = (grad - own * jnp.sum(own * grad, axis=-1, keepdims=True)) / length[...]
    columns = result.T
    part = columns.shape[0] // (N_YL * N_X * N_CORE)
    for yl in range(N_YL):
        for x in range(N_X):
            for core in range(N_CORE):
                at = ((yl * N_X + x) * N_CORE + core) * part
                turned[(yl * N_CORE + core) * N_X + x] = columns[at : at + part].astype(BF16)


def image_side_kernel(
    scale_log,
    logit_bias,
    img,
    unit,
    txt,
    txt_g,
    txt_b,
    txt_bg,
    turned,
    head,
    grad_out,
    loss_out,
    text_out,
):
    scale = jnp.exp(jnp.full((1, 1), scale_log[0], F32))
    bias = logit_bias[0]
    b, g, n_blk, n_group = homes()
    last_b = b - lax.rem(b + n_blk - 1, n_blk)
    last_g = g - lax.rem(g + n_group - 1, n_group)
    aparts = (0 * b, last_g, last_b * n_group, last_b * n_group + last_g)
    wide = img[...].astype(F32)
    size = lengths_of(wide)
    own = wide / size
    image = own.astype(BF16)
    total = jnp.zeros(wide.shape, F32)
    loss = jnp.zeros((wide.shape[0], 1), F32)
    own_code = split_block(txt)[1]
    for block, apart in zip((txt, txt_g, txt_b, txt_bg), aparts):
        feats, code = split_block(block)
        if block is txt:
            texts = unit[...].astype(BF16)
        else:
            pre = jnp.dot(feats, head[...], preferred_element_type=F32)
            texts = (pre / lengths_of(pre)).astype(BF16)
        match = met_pairs(own_code, code, apart, n_blk * n_group)
        value = signed_logit(dot_nt(image, texts), match, scale, bias)
        loss += jnp.sum(softplus(value), axis=-1, keepdims=True)
        total += jnp.dot(slope_of(value, match), texts, preferred_element_type=F32)
    grad = scale * total
    grad_out[...] = (grad - own * jnp.sum(own * grad, axis=-1, keepdims=True)) / size
    loss_out[...] = jnp.broadcast_to(loss, (loss.shape[0], loss.shape[0])).T[0:1]
    blocks = [
        turned[(yl * N_CORE + core) * N_X + x].astype(F32)
        for yl in range(N_YL)
        for x in range(N_X)
        for core in range(N_CORE)
    ]
    delta = jnp.concatenate(blocks, axis=0).T.astype(BF16)
    text_out[...] = dot_nt(delta, head[...])


def head_kernel(place, met, feats, feats_c, feats_y, feats_cy, out):
    m = place[0]
    across = m + 1 - 2 * lax.rem(m, 2)
    total = jnp.zeros((met.shape[1] * met.shape[2], feats.shape[1]), F32)
    for at, block in (
        (m, feats),
        (across, feats_c),
        (lax.rem(m + 2, 4), feats_y),
        (lax.rem(across + 2, 4), feats_cy),
    ):
        columns = met[at].astype(F32).reshape(total.shape[0], met.shape[3]).astype(BF16)
        total += jnp.dot(columns, block[...], preferred_element_type=F32)
    out[...] = total.reshape(out.shape).astype(BF16)


def pack_kernel(parts, out, wide, tail, packed):
    columns = jnp.sum(parts[...].astype(F32), axis=0)
    n, depth, lanes = wide.shape
    width = columns.shape[0]
    over = lanes - width
    left = width - over
    half = depth // 2
    wide[...] = jnp.concatenate([columns, columns[:over]], axis=0).T.reshape(wide.shape)
    copies = [columns[over:]] * (lanes // left)
    tail[...] = jnp.concatenate(copies, axis=0).T.reshape(tail.shape)
    lane = lax.broadcasted_iota(jnp.int32, (n, half, lanes), 2)
    packed[:, 0:half, :] = jnp.where(lane < width, wide[:, 0:half, :], wide[:, half:depth, :])
    short = half // 3
    lane = lax.broadcasted_iota(jnp.int32, (n, short, lanes), 2)
    rest = tail[:, half : half + short, :]
    for k in (1, 2):
        piece = tail[:, half + k * short : half + (k + 1) * short, :]
        rest = jnp.where(lane >= k * left, piece, rest)
    packed[:, half : half + short, :] = rest
    out[...] = packed[...].astype(BF16)


def unpack_kernel(parts, out):
    total = jnp.sum(parts[...].astype(F32), axis=0)
    depth, width = out.shape
    lanes = total.shape[1]
    over = lanes - width
    left = width - over
    half = depth // 2
    short = half // 3
    out[0:half, :] = total[0:half, 0:width]
    out[half:depth, 0:over] = total[0:half, width:lanes]
    for k in range(3):
        at = half + k * short
        out[at : at + short, over:width] = total[half : half + short, k * left : (k + 1) * left]


def body(image_emb, text_feats, text_head, scale_log, logit_bias, pair_index):
    rows, width = image_emb.shape
    n_blk = lax.axis_size(BLK)
    ids = pair_index.reshape(1, rows)
    like = jax.ShapeDtypeStruct
    score = 2 * rows * rows * width

    block = like((rows + 8, width), BF16)
    img, txt = kernel_call(
        block_kernel, (block, block), 0, (), (image_emb, text_feats, ids), vmem=60 * 1024 * 1024
    )
    img_b = shifted(img, BLK, -1)
    txt_b = shifted(txt, BLK, 1)
    swap = [(0, 1), (1, 0)]
    unit, length = kernel_call(
        text_kernel,
        (like((rows, width), F32), like((rows, 1), F32)),
        TEXT_FLOPS,
        (),
        (after(text_feats, img), text_head),
    )
    late_img, late_txt, late_feats = lax.optimization_barrier((img, txt, text_feats, unit))[:3]
    img_g = shifted(late_img, GROUP, -1)
    txt_g = shifted(late_txt, GROUP, 1)
    feats_c = lax.ppermute(late_feats, "core", swap)
    img_b, txt_b = lax.optimization_barrier((img_b, txt_b, unit, feats_c))[:2]
    img_bg = shifted(img_b, GROUP, -1)
    feats_y = lax.ppermute(after(text_feats, img_b), "yl", swap)

    part = width // (N_YL * N_X * N_CORE)
    turned = kernel_call(
        text_side_kernel,
        like((N_YL * N_CORE * N_X, part, rows), BF16),
        8 * score,
        (scale_log, logit_bias),
        (after(unit, txt_g), length, img, img_g, img_b, img_bg),
    )

    late_b = after(txt_b, turned)
    feats_cy = lax.ppermute(feats_y, "core", swap)
    txt_bg = shifted(late_b, GROUP, 1)
    place = lax.axis_index(QUAD).reshape(1)
    quads = turned.reshape(N_YL * N_CORE, N_X, part, rows)
    met = lax.all_to_all(quads, QUAD, 0, 0)
    products = kernel_call(
        head_kernel,
        like((N_X, part, width), BF16),
        2 * 4 * rows * width * N_X * part,
        (place,),
        (met, text_feats, feats_c, feats_y, feats_cy),
    )
    partial = lax.all_to_all(products, "x", 0, 0)
    image_grad, row_loss, text_grad = kernel_call(
        image_side_kernel,
        (like((rows, width), F32), like((1, rows), F32), like((rows, width), F32)),
        24 * score + 24 * rows * width * width,
        (scale_log, logit_bias),
        (
            after(image_emb, products),
            unit,
            txt,
            txt_g,
            txt_b,
            txt_bg,
            turned,
            text_head,
        ),
    )
    depth = width // n_blk
    packed = kernel_call(
        pack_kernel,
        like((n_blk, 16, 128), BF16),
        0,
        (),
        (partial,),
        (
            pltpu.VMEM((n_blk, depth, 128), F32),
            pltpu.VMEM((n_blk, depth, 128), F32),
            pltpu.VMEM((n_blk, 16, 128), F32),
        ),
    )
    packed = after(packed, row_loss)
    summed = lax.all_to_all(packed, BLK, 0, 0)
    head_grad = kernel_call(unpack_kernel, like((depth, part), F32), 0, (), (summed,))

    return (image_grad, text_grad, head_grad, row_loss.reshape(rows))


def solution(mesh):
    fine = Mesh(mesh.devices.reshape(4, 12, N_YL, N_X, N_CORE), ALL)
    rows = P(ALL, None)
    return jax.shard_map(
        body,
        mesh=fine,
        in_specs=(rows, rows, P(), P(), P(), P(ALL)),
        out_specs=(rows, rows, P(BLK, GROUP), P(ALL)),
        check_vma=False,
    )
```

```python
import jax
import jax.numpy as jnp
from jax import lax
from jax.experimental import pallas as pl
from jax.experimental.pallas import tpu as pltpu
from jax.sharding import Mesh
from jax.sharding import PartitionSpec as P

EPS = 1e-06
BF16 = jnp.bfloat16
F32 = jnp.float32
BLK = ("yh", "z")
GROUP = ("yl", "x", "core")
QUAD = ("yl", "core")
ALL = BLK + GROUP
N_YL, N_X, N_CORE = 2, 4, 2
TEXT_FLOPS = 12 * 10**9
VMEM_BYTES = 12 * 1024 * 1024


def shifted(value, axes, by):
    length = lax.axis_size(axes)
    return lax.ppermute(value, axes, [(i, (i + by) % length) for i in range(length)])


def kernel_call(
    kernel, out_shape, flops, scalars, arrays, scratch=(), vmem=VMEM_BYTES, left_out=0
):
    moved = sum(v.size * v.dtype.itemsize for v in arrays)
    moved += sum(v.size * v.dtype.itemsize for v in jax.tree.leaves(out_shape))
    return pl.pallas_call(
        kernel,
        out_shape=out_shape,
        in_specs=[pl.BlockSpec(memory_space=pltpu.SMEM)] * len(scalars)
        + [pl.BlockSpec(memory_space=pltpu.VMEM)] * (len(arrays) - left_out)
        + [pl.BlockSpec(memory_space=pl.ANY)] * left_out,
        out_specs=jax.tree.map(lambda _: pl.BlockSpec(memory_space=pltpu.VMEM), out_shape),
        scratch_shapes=scratch,
        compiler_params=pltpu.CompilerParams(vmem_limit_bytes=vmem),
        cost_estimate=pl.CostEstimate(flops=flops, bytes_accessed=moved, transcendentals=0),
    )(*scalars, *arrays)


def dot_nt(left, right):
    return lax.dot_general(left, right, (((1,), (1,)), ((), ())), preferred_element_type=F32)


def lengths_of(vectors):
    return jnp.sqrt(jnp.sum(vectors * vectors, axis=-1, keepdims=True) + EPS)


def after(value, *earlier):
    return lax.optimization_barrier((value,) + earlier)[0]


def homes():
    n_group = N_YL * N_X * N_CORE
    n_blk = lax.axis_size("yh") * lax.axis_size("z")
    b = lax.axis_index("yh") * lax.axis_size("z") + lax.axis_index("z")
    g = (lax.axis_index("yl") * N_X + lax.axis_index("x")) * N_CORE + lax.axis_index("core")
    return b, g, n_blk, n_group


def offsets_of(ids):
    b, g, n_blk, n_group = homes()
    rows = ids.shape[1]
    total = n_blk * n_group * rows
    own = (b * n_group + g) * rows + lax.broadcasted_iota(jnp.int32, ids.shape, 1)
    step = ids - own
    step = jnp.where(step < 0, step + total, step)
    code = jnp.where(step == 0, 0.0, float(n_group + 1))
    code = jnp.where(step == rows, 1.0, code)
    return jnp.where(step == n_group * rows, float(n_group), code)


def with_offsets(units, ids):
    code = jnp.broadcast_to(offsets_of(ids), (8, ids.shape[1]))
    rest = jnp.zeros((8, units.shape[1] - ids.shape[1]), F32)
    return jnp.concatenate([units, jnp.concatenate([code, rest], axis=1)], axis=0).astype(BF16)


def split_block(block):
    rows = block.shape[0] - 8
    code = block[...].astype(F32)[rows : rows + 1, 0:rows]
    return block[0:rows, :], code


def met_pairs(image_code, text_code, apart, total):
    rows = image_code.shape[1]
    row = lax.broadcasted_iota(jnp.int32, (rows, rows), 0)
    column = lax.broadcasted_iota(jnp.int32, (rows, rows), 1)
    step = image_code - text_code + apart.astype(F32)
    same = (step == 0.0) | (step == float(total)) | (step == -float(total))
    return (row == column) & same


def signed_logit(score, match, scale, bias):
    logit = scale * score + bias
    return jnp.where(match, -logit, logit)


def slope_of(value, match):
    slope = 1.0 / (1.0 + jnp.exp(-value))
    return jnp.where(match, -slope, slope).astype(BF16)


def softplus(value):
    return jnp.maximum(value, 0.0) + jnp.log1p(jnp.exp(-jnp.abs(value)))


def block_kernel(ids, img, feats, img_block, txt_block, img_buf, txt_buf, arrived):
    img_copy = pltpu.make_async_copy(img, img_buf, arrived.at[0])
    txt_copy = pltpu.make_async_copy(feats, txt_buf, arrived.at[1])
    img_copy.start()
    txt_copy.start()
    img_copy.wait()
    wide = img_buf[...].astype(F32)
    img_block[...] = with_offsets(wide / lengths_of(wide), ids[...])
    txt_copy.wait()
    txt_block[...] = with_offsets(txt_buf[...].astype(F32), ids[...])


def text_kernel(feats, head, unit, length):
    pre = jnp.dot(feats[...], head[...], preferred_element_type=F32)
    size = lengths_of(pre)
    unit[...] = pre / size
    length[...] = size


def text_side_kernel(scale_log, logit_bias, unit, length, img, img_g, img_b, img_bg, turned):
    scale = jnp.exp(jnp.full((1, 1), scale_log[0], F32))
    bias = logit_bias[0]
    b, g, n_blk, n_group = homes()
    next_b = lax.rem(b + 1, n_blk) - b
    next_g = lax.rem(g + 1, n_group) - g
    aparts = (0 * b, next_g, next_b * n_group, next_b * n_group + next_g)
    own = unit[...]
    text = own.astype(BF16)
    total = jnp.zeros(own.shape, F32)
    own_code = split_block(img)[1]
    for block, apart in zip((img, img_g, img_b, img_bg), aparts):
        images, code = split_block(block)
        match = met_pairs(code, own_code, apart, n_blk * n_group)
        value = signed_logit(dot_nt(text, images), match, scale, bias)
        total += jnp.dot(slope_of(value, match), images, preferred_element_type=F32)
    grad = scale * total
    result = (grad - own * jnp.sum(own * grad, axis=-1, keepdims=True)) / length[...]
    columns = result.T
    part = columns.shape[0] // (N_YL * N_X * N_CORE)
    for yl in range(N_YL):
        for x in range(N_X):
            for core in range(N_CORE):
                at = ((yl * N_X + x) * N_CORE + core) * part
                turned[(yl * N_CORE + core) * N_X + x] = columns[at : at + part].astype(BF16)


def image_side_kernel(
    scale_log,
    logit_bias,
    img,
    unit,
    txt,
    txt_g,
    txt_b,
    txt_bg,
    turned,
    head,
    grad_out,
    loss_out,
    text_out,
):
    scale = jnp.exp(jnp.full((1, 1), scale_log[0], F32))
    bias = logit_bias[0]
    b, g, n_blk, n_group = homes()
    last_b = b - lax.rem(b + n_blk - 1, n_blk)
    last_g = g - lax.rem(g + n_group - 1, n_group)
    aparts = (0 * b, last_g, last_b * n_group, last_b * n_group + last_g)
    wide = img[...].astype(F32)
    size = lengths_of(wide)
    own = wide / size
    image = own.astype(BF16)
    total = jnp.zeros(wide.shape, F32)
    loss = jnp.zeros((wide.shape[0], 1), F32)
    own_code = split_block(txt)[1]
    for block, apart in zip((txt, txt_g, txt_b, txt_bg), aparts):
        feats, code = split_block(block)
        if block is txt:
            texts = unit[...].astype(BF16)
        else:
            pre = jnp.dot(feats, head[...], preferred_element_type=F32)
            texts = (pre / lengths_of(pre)).astype(BF16)
        match = met_pairs(own_code, code, apart, n_blk * n_group)
        value = signed_logit(dot_nt(image, texts), match, scale, bias)
        loss += jnp.sum(softplus(value), axis=-1, keepdims=True)
        total += jnp.dot(slope_of(value, match), texts, preferred_element_type=F32)
    grad = scale * total
    grad_out[...] = (grad - own * jnp.sum(own * grad, axis=-1, keepdims=True)) / size
    loss_out[...] = jnp.broadcast_to(loss, (loss.shape[0], loss.shape[0])).T[0:1]
    blocks = [
        turned[(yl * N_CORE + core) * N_X + x].astype(F32)
        for yl in range(N_YL)
        for x in range(N_X)
        for core in range(N_CORE)
    ]
    delta = jnp.concatenate(blocks, axis=0).T.astype(BF16)
    text_out[...] = dot_nt(delta, head[...])


def head_kernel(place, met, feats_y, feats_cy, feats, feats_c, out, own_buf, core_buf, arrived):
    own_copy = pltpu.make_async_copy(feats, own_buf, arrived.at[0])
    core_copy = pltpu.make_async_copy(feats_c, core_buf, arrived.at[1])
    own_copy.start()
    core_copy.start()
    m = place[0]
    across = m + 1 - 2 * lax.rem(m, 2)

    def product(at, block):
        columns = met[at].astype(F32).reshape(-1, met.shape[3]).astype(BF16)
        return jnp.dot(columns, block[...], preferred_element_type=F32)

    total = product(lax.rem(m + 2, 4), feats_y)
    total += product(lax.rem(across + 2, 4), feats_cy)
    own_copy.wait()
    total += product(m, own_buf)
    core_copy.wait()
    total += product(across, core_buf)
    out[...] = total.reshape(out.shape).astype(BF16)


def pack_kernel(parts, out, wide, tail, packed):
    columns = jnp.sum(parts[...].astype(F32), axis=0)
    n, depth, lanes = wide.shape
    width = columns.shape[0]
    over = lanes - width
    left = width - over
    half = depth // 2
    wide[...] = jnp.concatenate([columns, columns[:over]], axis=0).T.reshape(wide.shape)
    copies = [columns[over:]] * (lanes // left)
    tail[...] = jnp.concatenate(copies, axis=0).T.reshape(tail.shape)
    lane = lax.broadcasted_iota(jnp.int32, (n, half, lanes), 2)
    packed[:, 0:half, :] = jnp.where(lane < width, wide[:, 0:half, :], wide[:, half:depth, :])
    short = half // 3
    lane = lax.broadcasted_iota(jnp.int32, (n, short, lanes), 2)
    rest = tail[:, half : half + short, :]
    for k in (1, 2):
        piece = tail[:, half + k * short : half + (k + 1) * short, :]
        rest = jnp.where(lane >= k * left, piece, rest)
    packed[:, half : half + short, :] = rest
    out[...] = packed[...].astype(BF16)


def unpack_kernel(parts, out):
    total = jnp.sum(parts[...].astype(F32), axis=0)
    depth, width = out.shape
    lanes = total.shape[1]
    over = lanes - width
    left = width - over
    half = depth // 2
    short = half // 3
    out[0:half, :] = total[0:half, 0:width]
    out[half:depth, 0:over] = total[0:half, width:lanes]
    for k in range(3):
        at = half + k * short
        out[at : at + short, over:width] = total[half : half + short, k * left : (k + 1) * left]


def body(image_emb, text_feats, text_head, scale_log, logit_bias, pair_index):
    rows, width = image_emb.shape
    n_blk = lax.axis_size(BLK)
    ids = pair_index.reshape(1, rows)
    like = jax.ShapeDtypeStruct
    score = 2 * rows * rows * width

    block = like((rows + 8, width), BF16)
    img, txt = kernel_call(
        block_kernel,
        (block, block),
        0,
        (),
        (ids, image_emb, text_feats),
        (
            pltpu.VMEM((rows, width), BF16),
            pltpu.VMEM((rows, width), BF16),
            pltpu.SemaphoreType.DMA((2,)),
        ),
        vmem=60 * 1024 * 1024,
        left_out=2,
    )
    img_b = shifted(img, BLK, -1)
    txt_b = shifted(txt, BLK, 1)
    swap = [(0, 1), (1, 0)]
    unit, length = kernel_call(
        text_kernel,
        (like((rows, width), F32), like((rows, 1), F32)),
        TEXT_FLOPS,
        (),
        (after(text_feats, img), text_head),
    )
    late_img, late_txt, late_feats = lax.optimization_barrier((img, txt, text_feats, unit))[:3]
    img_g = shifted(late_img, GROUP, -1)
    txt_g = shifted(late_txt, GROUP, 1)
    feats_c = lax.ppermute(late_feats, "core", swap)
    img_b, txt_b = lax.optimization_barrier((img_b, txt_b, unit, feats_c))[:2]
    img_bg = shifted(img_b, GROUP, -1)
    feats_y = lax.ppermute(after(text_feats, img_b), "yl", swap)

    part = width // (N_YL * N_X * N_CORE)
    turned = kernel_call(
        text_side_kernel,
        like((N_YL * N_CORE * N_X, part, rows), BF16),
        8 * score,
        (scale_log, logit_bias),
        (after(unit, txt_g), length, img, img_g, img_b, img_bg),
    )

    late_b = after(txt_b, turned)
    feats_cy = lax.ppermute(feats_y, "core", swap)
    txt_bg = shifted(late_b, GROUP, 1)
    place = lax.axis_index(QUAD).reshape(1)
    quads = turned.reshape(N_YL * N_CORE, N_X, part, rows)
    met = lax.all_to_all(quads, QUAD, 0, 0)
    products = kernel_call(
        head_kernel,
        like((N_X, part, width), BF16),
        2 * 4 * rows * width * N_X * part,
        (place,),
        (met, feats_y, feats_cy, text_feats, feats_c),
        (
            pltpu.VMEM((rows, width), BF16),
            pltpu.VMEM((rows, width), BF16),
            pltpu.SemaphoreType.DMA((2,)),
        ),
        left_out=2,
    )
    partial = lax.all_to_all(products, "x", 0, 0)
    image_grad, row_loss, text_grad = kernel_call(
        image_side_kernel,
        (like((rows, width), F32), like((1, rows), F32), like((rows, width), F32)),
        24 * score + 24 * rows * width * width,
        (scale_log, logit_bias),
        (
            after(image_emb, products),
            unit,
            txt,
            txt_g,
            txt_b,
            txt_bg,
            turned,
            text_head,
        ),
    )
    depth = width // n_blk
    packed = kernel_call(
        pack_kernel,
        like((n_blk, 16, 128), BF16),
        0,
        (),
        (partial,),
        (
            pltpu.VMEM((n_blk, depth, 128), F32),
            pltpu.VMEM((n_blk, depth, 128), F32),
            pltpu.VMEM((n_blk, 16, 128), F32),
        ),
    )
    packed = after(packed, row_loss)
    summed = lax.all_to_all(packed, BLK, 0, 0)
    head_grad = kernel_call(unpack_kernel, like((depth, part), F32), 0, (), (summed,))

    return (image_grad, text_grad, head_grad, row_loss.reshape(rows))


def solution(mesh):
    fine = Mesh(mesh.devices.reshape(4, 12, N_YL, N_X, N_CORE), ALL)
    rows = P(ALL, None)
    return jax.shard_map(
        body,
        mesh=fine,
        in_specs=(rows, rows, P(), P(), P(), P(ALL)),
        out_specs=(rows, rows, P(BLK, GROUP), P(ALL)),
        check_vma=False,
    )
```

```python
import jax
import jax.numpy as jnp
from jax import lax
from jax.experimental import pallas as pl
from jax.experimental.pallas import tpu as pltpu
from jax.sharding import Mesh
from jax.sharding import PartitionSpec as P

EPS = 1e-06
BF16 = jnp.bfloat16
F32 = jnp.float32
BLK = ("yh", "z")
GROUP = ("yl", "x", "core")
QUAD = ("yl", "core")
ALL = BLK + GROUP
N_YL, N_X, N_CORE = 2, 4, 2
TEXT_FLOPS = 12 * 10**9
VMEM_BYTES = 12 * 1024 * 1024


def shifted(value, axes, by):
    length = lax.axis_size(axes)
    return lax.ppermute(value, axes, [(i, (i + by) % length) for i in range(length)])


def kernel_call(
    kernel, out_shape, flops, scalars, arrays, scratch=(), vmem=VMEM_BYTES, left_out=0
):
    moved = sum(v.size * v.dtype.itemsize for v in arrays)
    moved += sum(v.size * v.dtype.itemsize for v in jax.tree.leaves(out_shape))
    return pl.pallas_call(
        kernel,
        out_shape=out_shape,
        in_specs=[pl.BlockSpec(memory_space=pltpu.SMEM)] * len(scalars)
        + [pl.BlockSpec(memory_space=pltpu.VMEM)] * (len(arrays) - left_out)
        + [pl.BlockSpec(memory_space=pl.ANY)] * left_out,
        out_specs=jax.tree.map(lambda _: pl.BlockSpec(memory_space=pltpu.VMEM), out_shape),
        scratch_shapes=scratch,
        compiler_params=pltpu.CompilerParams(vmem_limit_bytes=vmem),
        cost_estimate=pl.CostEstimate(flops=flops, bytes_accessed=moved, transcendentals=0),
    )(*scalars, *arrays)


def dot_nt(left, right):
    return lax.dot_general(left, right, (((1,), (1,)), ((), ())), preferred_element_type=F32)


def lengths_of(vectors):
    return jnp.sqrt(jnp.sum(vectors * vectors, axis=-1, keepdims=True) + EPS)


def after(value, *earlier):
    return lax.optimization_barrier((value,) + earlier)[0]


def homes():
    n_group = N_YL * N_X * N_CORE
    n_blk = lax.axis_size("yh") * lax.axis_size("z")
    b = lax.axis_index("yh") * lax.axis_size("z") + lax.axis_index("z")
    g = (lax.axis_index("yl") * N_X + lax.axis_index("x")) * N_CORE + lax.axis_index("core")
    return b, g, n_blk, n_group


def offsets_of(ids):
    b, g, n_blk, n_group = homes()
    rows = ids.shape[1]
    total = n_blk * n_group * rows
    own = (b * n_group + g) * rows + lax.broadcasted_iota(jnp.int32, ids.shape, 1)
    step = ids - own
    step = jnp.where(step < 0, step + total, step)
    code = jnp.where(step == 0, 0.0, float(n_group + 1))
    code = jnp.where(step == rows, 1.0, code)
    return jnp.where(step == n_group * rows, float(n_group), code)


def with_offsets(units, ids):
    code = jnp.broadcast_to(offsets_of(ids), (8, ids.shape[1]))
    rest = jnp.zeros((8, units.shape[1] - ids.shape[1]), F32)
    return jnp.concatenate([units, jnp.concatenate([code, rest], axis=1)], axis=0).astype(BF16)


def split_block(block):
    rows = block.shape[0] - 8
    code = block[...].astype(F32)[rows : rows + 1, 0:rows]
    return block[0:rows, :], code


def met_pairs(image_code, text_code, apart, total):
    rows = image_code.shape[1]
    row = lax.broadcasted_iota(jnp.int32, (rows, rows), 0)
    column = lax.broadcasted_iota(jnp.int32, (rows, rows), 1)
    step = image_code - text_code + apart.astype(F32)
    same = (step == 0.0) | (step == float(total)) | (step == -float(total))
    return (row == column) & same


def signed_logit(score, match, scale, bias):
    logit = scale * score + bias
    return jnp.where(match, -logit, logit)


def slope_of(value, match):
    slope = 1.0 / (1.0 + jnp.exp(-value))
    return jnp.where(match, -slope, slope).astype(BF16)


def softplus(value):
    return jnp.maximum(value, 0.0) + jnp.log1p(jnp.exp(-jnp.abs(value)))


def block_kernel(img, feats, ids, img_block, txt_block):
    wide = img[...].astype(F32)
    img_block[...] = with_offsets(wide / lengths_of(wide), ids[...])
    txt_block[...] = with_offsets(feats[...].astype(F32), ids[...])


def text_kernel(feats, head, unit, length):
    pre = jnp.dot(feats[...], head[...], preferred_element_type=F32)
    size = lengths_of(pre)
    unit[...] = pre / size
    length[...] = size


def text_side_kernel(scale_log, logit_bias, unit, length, img, img_g, img_b, img_bg, turned):
    scale = jnp.exp(jnp.full((1, 1), scale_log[0], F32))
    bias = logit_bias[0]
    b, g, n_blk, n_group = homes()
    next_b = lax.rem(b + 1, n_blk) - b
    next_g = lax.rem(g + 1, n_group) - g
    aparts = (0 * b, next_g, next_b * n_group, next_b * n_group + next_g)
    own = unit[...]
    text = own.astype(BF16)
    total = jnp.zeros(own.shape, F32)
    own_code = split_block(img)[1]
    for block, apart in zip((img, img_g, img_b, img_bg), aparts):
        images, code = split_block(block)
        match = met_pairs(code, own_code, apart, n_blk * n_group)
        value = signed_logit(dot_nt(text, images), match, scale, bias)
        total += jnp.dot(slope_of(value, match), images, preferred_element_type=F32)
    grad = scale * total
    result = (grad - own * jnp.sum(own * grad, axis=-1, keepdims=True)) / length[...]
    columns = result.T
    part = columns.shape[0] // (N_YL * N_X * N_CORE)
    for yl in range(N_YL):
        for x in range(N_X):
            for core in range(N_CORE):
                at = ((yl * N_X + x) * N_CORE + core) * part
                turned[(yl * N_CORE + core) * N_X + x] = columns[at : at + part].astype(BF16)


def image_side_kernel(
    scale_log,
    logit_bias,
    img,
    unit,
    txt,
    txt_g,
    txt_b,
    txt_bg,
    turned,
    head,
    grad_out,
    loss_out,
    text_out,
):
    scale = jnp.exp(jnp.full((1, 1), scale_log[0], F32))
    bias = logit_bias[0]
    b, g, n_blk, n_group = homes()
    last_b = b - lax.rem(b + n_blk - 1, n_blk)
    last_g = g - lax.rem(g + n_group - 1, n_group)
    aparts = (0 * b, last_g, last_b * n_group, last_b * n_group + last_g)
    wide = img[...].astype(F32)
    size = lengths_of(wide)
    own = wide / size
    image = own.astype(BF16)
    total = jnp.zeros(wide.shape, F32)
    loss = jnp.zeros((wide.shape[0], 1), F32)
    own_code = split_block(txt)[1]
    for block, apart in zip((txt, txt_g, txt_b, txt_bg), aparts):
        feats, code = split_block(block)
        if block is txt:
            texts = unit[...].astype(BF16)
        else:
            pre = jnp.dot(feats, head[...], preferred_element_type=F32)
            texts = (pre / lengths_of(pre)).astype(BF16)
        match = met_pairs(own_code, code, apart, n_blk * n_group)
        value = signed_logit(dot_nt(image, texts), match, scale, bias)
        loss += jnp.sum(softplus(value), axis=-1, keepdims=True)
        total += jnp.dot(slope_of(value, match), texts, preferred_element_type=F32)
    grad = scale * total
    grad_out[...] = (grad - own * jnp.sum(own * grad, axis=-1, keepdims=True)) / size
    loss_out[...] = jnp.broadcast_to(loss, (loss.shape[0], loss.shape[0])).T[0:1]
    blocks = [
        turned[(yl * N_CORE + core) * N_X + x].astype(F32)
        for yl in range(N_YL)
        for x in range(N_X)
        for core in range(N_CORE)
    ]
    delta = jnp.concatenate(blocks, axis=0).T.astype(BF16)
    text_out[...] = dot_nt(delta, head[...])


def head_kernel(place, met, feats_y, feats_cy, feats, feats_c, out, own_buf, core_buf, arrived):
    own_copy = pltpu.make_async_copy(feats, own_buf, arrived.at[0])
    core_copy = pltpu.make_async_copy(feats_c, core_buf, arrived.at[1])
    own_copy.start()
    core_copy.start()
    m = place[0]
    across = m + 1 - 2 * lax.rem(m, 2)

    def product(at, block):
        columns = met[at].astype(F32).reshape(-1, met.shape[3]).astype(BF16)
        return jnp.dot(columns, block[...], preferred_element_type=F32)

    total = product(lax.rem(m + 2, 4), feats_y)
    total += product(lax.rem(across + 2, 4), feats_cy)
    own_copy.wait()
    total += product(m, own_buf)
    core_copy.wait()
    total += product(across, core_buf)
    out[...] = total.reshape(out.shape).astype(BF16)


def pack_kernel(parts, out, wide, tail, packed):
    columns = jnp.sum(parts[...].astype(F32), axis=0)
    n, depth, lanes = wide.shape
    width = columns.shape[0]
    over = lanes - width
    left = width - over
    half = depth // 2
    wide[...] = jnp.concatenate([columns, columns[:over]], axis=0).T.reshape(wide.shape)
    copies = [columns[over:]] * (lanes // left)
    tail[...] = jnp.concatenate(copies, axis=0).T.reshape(tail.shape)
    lane = lax.broadcasted_iota(jnp.int32, (n, half, lanes), 2)
    packed[:, 0:half, :] = jnp.where(lane < width, wide[:, 0:half, :], wide[:, half:depth, :])
    short = half // 3
    lane = lax.broadcasted_iota(jnp.int32, (n, short, lanes), 2)
    rest = tail[:, half : half + short, :]
    for k in (1, 2):
        piece = tail[:, half + k * short : half + (k + 1) * short, :]
        rest = jnp.where(lane >= k * left, piece, rest)
    packed[:, half : half + short, :] = rest
    out[...] = packed[...].astype(BF16)


def unpack_kernel(parts, out):
    total = jnp.sum(parts[...].astype(F32), axis=0)
    depth, width = out.shape
    lanes = total.shape[1]
    over = lanes - width
    left = width - over
    half = depth // 2
    short = half // 3
    out[0:half, :] = total[0:half, 0:width]
    out[half:depth, 0:over] = total[0:half, width:lanes]
    for k in range(3):
        at = half + k * short
        out[at : at + short, over:width] = total[half : half + short, k * left : (k + 1) * left]


def body(image_emb, text_feats, text_head, scale_log, logit_bias, pair_index):
    rows, width = image_emb.shape
    n_blk = lax.axis_size(BLK)
    ids = pair_index.reshape(1, rows)
    like = jax.ShapeDtypeStruct
    score = 2 * rows * rows * width

    block = like((rows + 8, width), BF16)
    img, txt = kernel_call(
        block_kernel, (block, block), 0, (), (image_emb, text_feats, ids), vmem=60 * 1024 * 1024
    )
    img_b = shifted(img, BLK, -1)
    txt_b = shifted(txt, BLK, 1)
    swap = [(0, 1), (1, 0)]
    feats_c = lax.ppermute(after(text_feats, img), "core", swap)
    unit, length = kernel_call(
        text_kernel,
        (like((rows, width), F32), like((rows, 1), F32)),
        TEXT_FLOPS,
        (),
        (after(text_feats, feats_c), text_head),
    )
    late_img, late_txt = lax.optimization_barrier((img, txt, feats_c))[:2]
    img_g = shifted(late_img, GROUP, -1)
    txt_g = shifted(late_txt, GROUP, 1)
    img_b = after(img_b, unit, feats_c)
    img_bg = shifted(img_b, GROUP, -1)
    feats_y = lax.ppermute(after(text_feats, img_b), "yl", swap)

    part = width // (N_YL * N_X * N_CORE)
    turned = kernel_call(
        text_side_kernel,
        like((N_YL * N_CORE * N_X, part, rows), BF16),
        8 * score,
        (scale_log, logit_bias),
        (after(unit, txt_b, txt_g), length, img, img_g, img_b, img_bg),
    )

    late_b = after(txt_b, turned)
    feats_cy = lax.ppermute(feats_y, "core", swap)
    txt_bg = shifted(late_b, GROUP, 1)
    place = lax.axis_index(QUAD).reshape(1)
    quads = turned.reshape(N_YL * N_CORE, N_X, part, rows)
    met = lax.all_to_all(quads, QUAD, 0, 0)
    products = kernel_call(
        head_kernel,
        like((N_X, part, width), BF16),
        2 * 4 * rows * width * N_X * part,
        (place,),
        (met, feats_y, feats_cy, text_feats, feats_c),
        (
            pltpu.VMEM((rows, width), BF16),
            pltpu.VMEM((rows, width), BF16),
            pltpu.SemaphoreType.DMA((2,)),
        ),
        left_out=2,
    )
    partial = lax.all_to_all(products, "x", 0, 0)
    image_grad, row_loss, text_grad = kernel_call(
        image_side_kernel,
        (like((rows, width), F32), like((1, rows), F32), like((rows, width), F32)),
        24 * score + 24 * rows * width * width,
        (scale_log, logit_bias),
        (
            after(image_emb, products),
            unit,
            txt,
            txt_g,
            txt_b,
            txt_bg,
            turned,
            text_head,
        ),
    )
    depth = width // n_blk
    packed = kernel_call(
        pack_kernel,
        like((n_blk, 16, 128), BF16),
        0,
        (),
        (partial,),
        (
            pltpu.VMEM((n_blk, depth, 128), F32),
            pltpu.VMEM((n_blk, depth, 128), F32),
            pltpu.VMEM((n_blk, 16, 128), F32),
        ),
    )
    packed = after(packed, row_loss)
    summed = lax.all_to_all(packed, BLK, 0, 0)
    head_grad = kernel_call(unpack_kernel, like((depth, part), F32), 0, (), (summed,))

    return (image_grad, text_grad, head_grad, row_loss.reshape(rows))


def solution(mesh):
    fine = Mesh(mesh.devices.reshape(4, 12, N_YL, N_X, N_CORE), ALL)
    rows = P(ALL, None)
    return jax.shard_map(
        body,
        mesh=fine,
        in_specs=(rows, rows, P(), P(), P(), P(ALL)),
        out_specs=(rows, rows, P(BLK, GROUP), P(ALL)),
        check_vma=False,
    )
```
